128 devices in a mesh: tm: 8 (over y, core), video: 16 (over x, z).
Axes of the slice: x: 4, y: 4, z: 4, core: 2. Of those that a mesh axis runs over, the one named last changes fastest.
Arguments:
- frame_feats: bfloat16 [128, 128, 32, 768], P('tm', 'video'), may hold values from -192 to 192
- selected: int32 [128, 64], P('tm'), may hold values from 0 to 127, as said below
- counts: int32 [128], P('tm'), may hold values from 8 to 64, as said below
- video_start: int32 [128], replicated, may hold values from 0 to 32736, as said below
- queries: bfloat16 [32, 768], replicated, may hold values from -6 to 6
- frame_pos: bfloat16 [64, 768], replicated, may hold values from -6 to 6
- w_query: bfloat16 [768, 768], replicated, may hold values from -0.21875 to 0.21875
- w_key: bfloat16 [768, 768], replicated, may hold values from -0.21875 to 0.21875
- w_value: bfloat16 [768, 768], replicated, may hold values from -0.21875 to 0.21875
- w_out: bfloat16 [768, 768], replicated, may hold values from -0.21875 to 0.21875
- ln_gain: float32 [768], replicated, may hold values from 0.1 to 1.9
- ln_bias: float32 [768], replicated, may hold values from -3 to 3
- proj_weight: bfloat16 [768, 5120], P(None, 'tm'), may hold values from -0.21875 to 0.21875
- proj_bias: float32 [5120], replicated, may hold values from -3 to 3
- text_embeds: bfloat16 [32768, 5120], P(('tm', 'video')), may hold values from -6 to 6
- norm_gain: float32 [5120], replicated, may hold values from 0.1 to 1.9
Outputs:
- normed: bfloat16 [32768, 5120], P(('tm', 'video'))
The draws below stay inside these ranges and needn't reach their ends.
Inputs may be any that keep to these rules, and one draw needn't show every extreme that they name: Entry k < counts[w] of video w is a frame of the k-th of counts[w] equal intervals of its 128 frames; later entries are 0. So at most 4 selected frames of one video lie among one device's 8 frames of it, and every draw has a video with 64 selected frames. `counts`: each count is 8 times a power of two; some video has 64 in every draw. `video_start`: the 32 tokens of video w occupy consecutive positions of sequence w // 16 (positions s * 4096 to (s + 1) * 4096 of all, for sequence s), all inside one block of 256 positions k * 256 to (k + 1) * 256 of that sequence; each such block holds the tokens of exactly one video.
All inputs are finite; a program needn't handle non-finite values.
Results may differ from the reference program's by a relative error of at most 0.012.
Values may be sent and summed in bfloat16 or wider, within the bound.
No kernel may reach another device: no remote copies, remote signals or barrier semaphores. Data moves between devices by JAX's collectives and lax.ppermute only.
A program may use at most 128 MiB of HBM per device.

```python
import math
import jax
import jax.numpy as jnp
from jax import lax

DQ = 768
HEADS = 12
HD = 64
VQ = 32
QF = 32
DL = 5120
SEL = 64
FRAMES = 128
TOK_DEV = 256
VIDEOS = 128
SEQ_LEN = 4096
TOKENS = 32768
N_TM = 8
N_VIDEO = 16


def choose_counts(key):
    level_key = jax.random.fold_in(key, 101)
    first_draw = jax.random.randint(jax.random.fold_in(level_key, 1), (VIDEOS,), 0, 4)
    second = jax.random.randint(jax.random.fold_in(level_key, 2), (VIDEOS,), 0, 4)
    levels = jnp.maximum(first_draw, second)
    forced = jax.random.randint(jax.random.fold_in(level_key, 3), (), 0, VIDEOS)
    levels = jnp.where(jnp.arange(VIDEOS) == forced, 3, levels)
    return (8 * jnp.left_shift(1, levels)).astype(jnp.int32)


def draw_counts(key, part):
    shared = choose_counts(key)
    return shared


def draw_selected(key, part):
    shared = choose_counts(key)
    key = jax.random.fold_in(key, 5)
    stride = FRAMES // shared
    jitter = jax.random.randint(key, (VIDEOS, SEL), 0, FRAMES) % stride[:, None]
    slot_index = jnp.arange(SEL)[None, :]
    picked = jnp.where(slot_index < shared[:, None], slot_index * stride[:, None] + jitter, 0)
    return picked.astype(jnp.int32)


def draw_video_start(key, part):
    key = jax.random.fold_in(key, 7)
    video_ids = jnp.arange(VIDEOS, dtype=jnp.int32)
    sequence = video_ids // N_VIDEO
    column = video_ids % N_VIDEO
    half_way = N_VIDEO // 2
    special = jax.random.randint(jax.random.fold_in(key, 1), (N_TM,), 0, N_VIDEO)
    special_here = special[sequence]
    other_block = (special_here - 1 - half_way) % N_VIDEO
    block = (column - half_way) % N_VIDEO
    block = jnp.where(column == (special_here - 1) % N_VIDEO, special_here, jnp.where(column == (special_here + half_way) % N_VIDEO, other_block, block))
    spread = jax.random.randint(jax.random.fold_in(key, 2), (VIDEOS,), 0, TOK_DEV - VQ + 1)
    spread = jnp.where(block == 0, 0, jnp.where(block == N_VIDEO - 1, TOK_DEV - VQ, spread))
    return (sequence * SEQ_LEN + block * TOK_DEV + spread).astype(jnp.int32)


def scaled_frames(key, lowest, highest):
    base = jnp.clip(jax.random.normal(jax.random.fold_in(key, 1), (VIDEOS, FRAMES, QF, DQ), jnp.float32), -3.0, 3.0)
    scale = jnp.exp(jax.random.uniform(jax.random.fold_in(key, 2), (VIDEOS, FRAMES, 1, 1), jnp.float32, math.log(lowest), math.log(highest)))
    return base * scale


def draw_frame_feats(key, part):
    key = jax.random.fold_in(key, 9)
    return scaled_frames(key, 0.5, 2.0).astype(jnp.bfloat16)


def block_levels(own_key, shape, pieces, smallest, largest):
    def one(axis_at, blocks):
        heights = jax.random.uniform(jax.random.fold_in(jax.random.fold_in(own_key, 6), axis_at), (blocks,), jnp.float32, smallest / len(pieces), largest / len(pieces))
        return jnp.repeat(jnp.exp(heights), shape[axis_at] // blocks).reshape((-1,) + (1,) * (len(shape) - axis_at - 1))

    level = one(*pieces[0])
    for cut in pieces[1:]:
        level = level * one(*cut)
    return level


def bell_draw(stream_key, dims, width, reach, cuts=(), kind=jnp.bfloat16):
    gain = block_levels(stream_key, dims, cuts, -0.22, 0.18) if cuts else 1.0
    array = jax.random.normal(stream_key, dims, jnp.float32) * width * gain
    return jnp.minimum(jnp.maximum(array, -reach), reach).astype(kind)


def setup_inputs(seed: int = 0) -> dict:
    arg_keys = jax.random.split(jax.random.key(seed), 17)
    return {
        "frame_feats": draw_frame_feats(jax.random.fold_in(arg_keys[16], 71), 0),
        "selected": draw_selected(jax.random.fold_in(arg_keys[16], 71), 0),
        "counts": draw_counts(jax.random.fold_in(arg_keys[16], 71), 0),
        "video_start": draw_video_start(jax.random.fold_in(arg_keys[16], 71), 0),
        "queries": bell_draw(arg_keys[4], (VQ, DQ), 1.0, 6.0),
        "frame_pos": bell_draw(arg_keys[5], (SEL, DQ), 1.0, 6.0),
        "w_query": bell_draw(arg_keys[6], (DQ, DQ), DQ ** -0.5, 0.21875),
        "w_key": bell_draw(arg_keys[7], (DQ, DQ), DQ ** -0.5, 0.21875),
        "w_value": bell_draw(arg_keys[8], (DQ, DQ), DQ ** -0.5, 0.21875),
        "w_out": bell_draw(arg_keys[9], (DQ, DQ), DQ ** -0.5, 0.21875),
        "ln_gain": jnp.clip(1.0 + 0.18 * jax.random.normal(arg_keys[10], (DQ,), jnp.float32), 0.1, 1.9),
        "ln_bias": bell_draw(arg_keys[11], (DQ,), 0.5, 3.0, (), jnp.float32),
        "proj_weight": bell_draw(arg_keys[12], (DQ, DL), DQ ** -0.5, 0.21875, ((1, 8),)),
        "proj_bias": bell_draw(arg_keys[13], (DL,), 0.5, 3.0, (), jnp.float32),
        "text_embeds": bell_draw(arg_keys[14], (TOKENS, DL), 1.0, 6.0, ((0, 128),)),
        "norm_gain": jnp.clip(1.0 + 0.18 * jax.random.normal(arg_keys[15], (DL,), jnp.float32), 0.1, 1.9),
    }


def one_video(frames, frame_picks, frame_count, queries, frame_pos, query_vec, w_key, w_value, w_out, ln_gain, ln_bias):
    chosen = jnp.take(frames, frame_picks, axis=0)
    key_input = (chosen.astype(jnp.float32) + frame_pos.astype(jnp.float32)[:, None, :]).astype(jnp.bfloat16)
    key_input = key_input.reshape(SEL * QF, DQ)
    key_rows = jnp.dot(key_input, w_key, preferred_element_type=jnp.float32).astype(jnp.bfloat16)
    value_rows = jnp.dot(key_input, w_value, preferred_element_type=jnp.float32).astype(jnp.bfloat16)
    key_live = jnp.arange(SEL * QF, dtype=jnp.int32) // QF < frame_count
    scores = jnp.einsum('ihd,nhd->hin', query_vec.astype(jnp.float32).reshape(VQ, HEADS, HD), key_rows.astype(jnp.float32).reshape(SEL * QF, HEADS, HD)) * (1.0 / math.sqrt(HD))
    scores = jnp.where(key_live[None, None, :], scores, -jnp.inf)
    row_max = lax.optimization_barrier(jnp.max(scores, axis=-1, keepdims=True))
    weights_raw = jnp.exp(scores - row_max)
    probabilities = (weights_raw / lax.optimization_barrier(jnp.sum(weights_raw, axis=-1, keepdims=True))).astype(jnp.bfloat16)
    context = jnp.einsum('hin,nhd->ihd', probabilities.astype(jnp.float32), value_rows.astype(jnp.float32).reshape(SEL * QF, HEADS, HD))
    context = context.reshape(VQ, DQ).astype(jnp.bfloat16)
    residual = jnp.dot(context, w_out, preferred_element_type=jnp.float32) + queries.astype(jnp.float32)
    row_mean = lax.optimization_barrier(jnp.mean(residual, axis=-1, keepdims=True))
    variance = lax.optimization_barrier(jnp.mean(jnp.square(residual - row_mean), axis=-1, keepdims=True))
    return ((residual - row_mean) * lax.rsqrt(variance + 1e-12) * ln_gain + ln_bias).astype(jnp.bfloat16)

def reference(frame_feats, selected, counts, video_start, queries, frame_pos, w_query, w_key, w_value, w_out, ln_gain, ln_bias, proj_weight, proj_bias, text_embeds, norm_gain):
    query_vec = jnp.dot(queries, w_query, preferred_element_type=jnp.float32).astype(jnp.bfloat16)

    def per_video(packed):
        frames, frame_picks, frame_count = packed
        return one_video(frames, frame_picks, frame_count, queries, frame_pos, query_vec, w_key, w_value, w_out, ln_gain, ln_bias)
    video_out = lax.map(per_video, (frame_feats, selected, counts))
    projected = jnp.dot(video_out.reshape(VIDEOS * VQ, DQ), proj_weight, preferred_element_type=jnp.float32)
    projected = projected + proj_bias.astype(jnp.float32)
    row_ids = (video_start[:, None] + jnp.arange(VQ, dtype=jnp.int32)[None, :]).reshape(-1).astype(jnp.int32)
    embeds = text_embeds.astype(jnp.float32).at[row_ids].set(projected).astype(jnp.bfloat16)
    wide = embeds.astype(jnp.float32)
    squares = lax.optimization_barrier(jnp.mean(wide * wide, axis=-1, keepdims=True))
    return (wide * lax.rsqrt(squares + 1e-05) * norm_gain).astype(jnp.bfloat16)
```

```python
import math

import jax
import jax.numpy as jnp
from jax import lax
from jax.experimental import pallas as pl
from jax.experimental.pallas import tpu as pltpu
from jax.sharding import PartitionSpec as P

HEADS = 12
HD = 64
WIDTH = HEADS * HD
VQ = 32
QF = 32
DL = 5120
SLOTS = 4
COLUMNS = 16
BLOCK = 256
WINDOW = 48
STATS = 128
CHUNK = 4
GROUP = 4
NEG = -1e30
MIB = 1 << 20

f32 = jnp.float32
bf16 = jnp.bfloat16


def iota(shape, axis):
    return lax.broadcasted_iota(jnp.int32, shape, axis)


def attend_kernel(
    selected_in, counts_in, starts_in, frames, pos_in, queries_in, w_query_in, w_key_in, w_value_in, out,
    selected, counts, starts, pos, queries, w_query, w_key, w_value, x_raw, x_keys, folded, pos_wide,
    scalar_sems, sems, weight_sems,
):
    row = lax.axis_index("tm")
    column = lax.axis_index("video")
    scalars = [
        pltpu.make_async_copy(source, target, scalar_sems.at[i])
        for i, (source, target) in enumerate(
            ((selected_in, selected), (counts_in, counts), (starts_in, starts))
        )
    ]
    loads = [
        pltpu.make_async_copy(source, target, weight_sems.at[i])
        for i, (source, target) in enumerate((
            (queries_in, queries), (w_query_in, w_query), (w_key_in, w_key), (pos_in, pos),
            (w_value_in, w_value),
        ))
    ]
    for copy in scalars + loads:
        copy.start()
    for copy in scalars:
        copy.wait()

    def slot(video, j):
        count = counts[video]
        last = jnp.maximum(count >> 4, 1) - 1
        k = ((column * count) >> 4) + jnp.minimum(j, last)
        frame = selected[video, k] - column * 8
        live = (j <= last) & (frame >= 0) & (frame < 8)
        return k, jnp.clip(frame, 0, 7), live

    @pl.loop(0, COLUMNS)
    def _(video):
        for j in range(SLOTS):
            _, frame, _ = slot(video, j)
            pltpu.make_async_copy(
                frames.at[video, frame], x_raw.at[video * SLOTS + j], sems.at[video]
            ).start()

    for copy in loads[:3]:
        copy.wait()
    query = jnp.dot(queries[...], w_query[...], preferred_element_type=f32).astype(bf16)
    query = query * jnp.asarray(1.0 / math.sqrt(HD), bf16)
    for g in range(HEADS // GROUP):
        wide = GROUP * HD
        part = query[:, g * wide:(g + 1) * wide]
        part = jnp.concatenate([part] * GROUP, axis=0)
        same = iota(part.shape, 0) // VQ == iota(part.shape, 1) // HD
        part = jnp.where(same, part, jnp.zeros_like(part))
        fold = lax.dot_general(
            part, w_key[:, g * wide:(g + 1) * wide], (((1,), (1,)), ((), ())),
            preferred_element_type=f32,
        )
        high = fold.astype(bf16)
        rows = GROUP * VQ
        folded[g * rows:(g + 1) * rows, :] = high
        folded[HEADS * VQ + g * rows:HEADS * VQ + (g + 1) * rows, :] = (
            fold - high.astype(f32)
        ).astype(bf16)
    for copy in loads[3:]:
        copy.wait()
    pos_wide[...] = pos[...].astype(f32)

    lane = iota((VQ, STATS), 1)
    stat_head = lane % HEADS
    stat_part = lane // HEADS
    piece = stat_part % 3

    @pl.loop(0, COLUMNS // CHUNK)
    def _(chunk):
        lives = []
        for t in range(CHUNK):
            video = chunk * CHUNK + t
            pltpu.make_async_copy(
                frames.at[video, pl.ds(0, SLOTS)], x_raw.at[pl.ds(video * SLOTS, SLOTS)], sems.at[video]
            ).wait()
            alive = jnp.int32(0)
            for j in range(SLOTS):
                k, _, live = slot(video, j)
                alive = alive + live.astype(jnp.int32)
                x = x_raw[video * SLOTS + j].astype(f32) + pos_wide[pl.ds(k, 1), :]
                at = (t * SLOTS + j) * QF
                x_keys[at:at + QF, :] = x.astype(bf16)
            lives.append(alive)
        x = x_keys[...]
        both = lax.dot_general(folded[...], x, (((1,), (1,)), ((), ())), preferred_element_type=f32)
        scores = both[:HEADS * VQ] + both[HEADS * VQ:]
        values = jnp.dot(x, w_value[...], preferred_element_type=f32).astype(bf16)
        keys = SLOTS * QF
        for t in range(CHUNK):
            video = chunk * CHUNK + t
            hidden = jnp.where(iota((1, keys), 1) < lives[t] * QF, 0.0, NEG)
            s = scores[:, t * keys:(t + 1) * keys] + hidden
            top = jnp.max(s, axis=1, keepdims=True)
            p = jnp.exp(s - top)
            total = jnp.sum(p, axis=1, keepdims=True)
            p = p.astype(bf16)
            block = ((starts[row * COLUMNS + video] - row * (COLUMNS * BLOCK)) >> 8) & (COLUMNS - 1)
            for g in range(HEADS // GROUP):
                wide = GROUP * HD
                rows = GROUP * VQ
                full = jnp.dot(
                    p[g * rows:(g + 1) * rows], values[t * keys:(t + 1) * keys, g * wide:(g + 1) * wide],
                    preferred_element_type=f32,
                )
                head = iota((VQ, wide), 1) // HD
                context = full[:VQ]
                for h in range(1, GROUP):
                    context = jnp.where(head == h, full[h * VQ:(h + 1) * VQ], context)
                out[block, :, g * wide:(g + 1) * wide] = context.astype(bf16)
            stat = jnp.zeros((VQ, STATS), f32)
            for h in range(HEADS):
                one = jnp.where(stat_part < 3, top[h * VQ:(h + 1) * VQ], total[h * VQ:(h + 1) * VQ])
                stat = jnp.where(stat_head == h, one, stat)
            high = stat.astype(bf16).astype(f32)
            mid = (stat - high).astype(bf16).astype(f32)
            low = stat - high - mid
            stat = jnp.where(piece == 0, high, jnp.where(piece == 1, mid, low))
            stat = jnp.where(stat_part < 6, stat, 0.0)
            out[block, :, WIDTH:] = stat.astype(bf16)


def attend(selected, counts, starts, frames, pos, queries, w_query, w_key, w_value):
    return pl.pallas_call(
        attend_kernel,
        out_shape=jax.ShapeDtypeStruct((COLUMNS, VQ, WIDTH + STATS), bf16),
        in_specs=[pl.BlockSpec(memory_space=pl.ANY)] * 9,
        out_specs=pl.BlockSpec(memory_space=pltpu.VMEM),
        scratch_shapes=[
            pltpu.SMEM(selected.shape, jnp.int32),
            pltpu.SMEM(counts.shape, jnp.int32),
            pltpu.SMEM(starts.shape, jnp.int32),
            pltpu.VMEM(pos.shape, bf16),
            pltpu.VMEM(queries.shape, bf16),
            pltpu.VMEM((WIDTH, WIDTH), bf16),
            pltpu.VMEM((WIDTH, WIDTH), bf16),
            pltpu.VMEM((WIDTH, WIDTH), bf16),
            pltpu.VMEM((COLUMNS * SLOTS, QF, WIDTH), bf16),
            pltpu.VMEM((CHUNK * SLOTS * QF, WIDTH), bf16),
            pltpu.VMEM((2 * HEADS * VQ, WIDTH), bf16),
            pltpu.VMEM(pos.shape, f32),
            pltpu.SemaphoreType.DMA((3,)),
            pltpu.SemaphoreType.DMA((COLUMNS,)),
            pltpu.SemaphoreType.DMA((5,)),
        ],
        compiler_params=pltpu.CompilerParams(vmem_limit_bytes=60 * MIB),
        cost_estimate=pl.CostEstimate(
            flops=9_000_000_000, bytes_accessed=8_000_000, transcendentals=800_000
        ),
        name="attend",
    )(selected, counts, starts, frames, pos, queries, w_query, w_key, w_value)


def combine_kernel(parts, queries, w_out, gain, bias, out):
    stat = parts[:, :, WIDTH:].astype(f32).reshape(COLUMNS * VQ, STATS)

    def shifted(n):
        return pltpu.roll(stat, STATS - n * HEADS, 1)

    tops = stat + shifted(1) + shifted(2)
    totals = shifted(3) + shifted(4) + shifted(5)
    lane = iota((VQ, STATS), 1)
    real = lane < HEADS
    tops = [jnp.where(real, tops[c * VQ:(c + 1) * VQ], 0.0) for c in range(COLUMNS)]
    totals = [jnp.where(real, totals[c * VQ:(c + 1) * VQ], 1.0) for c in range(COLUMNS)]
    top = tops[0]
    for c in range(1, COLUMNS):
        top = jnp.maximum(top, tops[c])
    scales = [jnp.exp(t - top) for t in tops]
    total = scales[0] * totals[0]
    for c in range(1, COLUMNS):
        total = total + scales[c] * totals[c]
    inverse = jnp.where(real, 1.0 / total, 0.0)
    weight = jnp.concatenate([s * inverse for s in scales], axis=0)
    high = weight.astype(bf16)
    low = (weight - high.astype(f32)).astype(bf16)
    spread = (iota((2 * STATS, WIDTH), 0) % STATS == iota((2 * STATS, WIDTH), 1) // HD).astype(f32).astype(bf16)
    weight = jnp.dot(jnp.concatenate([high, low], axis=1), spread, preferred_element_type=f32)
    context = jnp.zeros((VQ, WIDTH), f32)
    for c in range(COLUMNS):
        context = context + weight[c * VQ:(c + 1) * VQ] * parts[c, :, :WIDTH].astype(f32)
    residual = jnp.dot(context.astype(bf16), w_out[...], preferred_element_type=f32) + queries[...].astype(f32)
    mean = jnp.mean(residual, axis=-1, keepdims=True)
    centred = residual - mean
    variance = jnp.mean(centred * centred, axis=-1, keepdims=True)
    out[...] = (centred * lax.rsqrt(variance + 1e-12) * gain[...] + bias[...]).astype(bf16)


def combine(parts, queries, w_out, gain, bias):
    vmem = pl.BlockSpec(memory_space=pltpu.VMEM)
    return pl.pallas_call(
        combine_kernel,
        out_shape=jax.ShapeDtypeStruct((VQ, WIDTH), bf16),
        in_specs=[vmem] * 5,
        out_specs=vmem,
        compiler_params=pltpu.CompilerParams(vmem_limit_bytes=24 * MIB),
        name="combine",
    )(parts, queries, w_out, gain.reshape(1, WIDTH), bias.reshape(1, WIDTH))


def project_kernel(rows, w0, w1, w2, w3, bias, out):
    here = lax.axis_index("tm")
    half = here // 4
    wide = w0.shape[1]
    for j, w in enumerate((w0, w1, w2, w3)):
        at = pl.multiple_of(((here % 4) ^ j) * wide, 128)
        shift = pl.multiple_of(half * (4 * wide) + at, 128)
        result = jnp.dot(rows[...], w[...], preferred_element_type=f32) + bias[:, pl.ds(shift, wide)]
        out[:, pl.ds(at, wide)] = result.astype(bf16)


def project(rows, weights, bias):
    vmem = pl.BlockSpec(memory_space=pltpu.VMEM)
    return pl.pallas_call(
        project_kernel,
        out_shape=jax.ShapeDtypeStruct((VQ, DL // 2), bf16),
        in_specs=[vmem] * 6,
        out_specs=vmem,
        compiler_params=pltpu.CompilerParams(vmem_limit_bytes=24 * MIB),
        cost_estimate=pl.CostEstimate(flops=126_000_000, bytes_accessed=4_200_000, transcendentals=0),
        name="project",
    )(rows, *weights, bias)


def norm_rows(wide, gain):
    squares = jnp.mean(wide * wide, axis=-1, keepdims=True)
    return (wide * lax.rsqrt(squares + 1e-05) * gain).astype(bf16)


def text_kernel(text, gain, out):
    out[...] = norm_rows(text[...].astype(f32), gain[...])


def norm_text(text, gain):
    rows = 64
    return pl.pallas_call(
        text_kernel,
        out_shape=jax.ShapeDtypeStruct(text.shape, bf16),
        grid=(text.shape[0] // rows,),
        in_specs=[
            pl.BlockSpec((rows, DL), lambda i: (i, 0)),
            pl.BlockSpec((1, DL), lambda i: (0, 0)),
        ],
        out_specs=pl.BlockSpec((rows, DL), lambda i: (i, 0)),
        compiler_params=pltpu.CompilerParams(vmem_limit_bytes=24 * MIB),
        cost_estimate=pl.CostEstimate(flops=8_000_000, bytes_accessed=5_300_000, transcendentals=256),
        name="norm_text",
    )(text, gain)


def place_kernel(starts, mine, other, gain, text, normed, out, text_rows, embeds, done_rows, sems):
    row = lax.axis_index("tm")
    column = lax.axis_index("video")
    first = (row * COLUMNS + column) * BLOCK
    offset = jnp.int32(0)
    for w in range(COLUMNS):
        at = starts[row * COLUMNS + w] - first
        offset = offset + jnp.where((at >= 0) & (at < BLOCK), at, 0)
    begin = pl.multiple_of(jnp.minimum(offset >> 4, (BLOCK - WINDOW) // 16) * 16, 16)
    fetch = pltpu.make_async_copy(text.at[pl.ds(begin, WINDOW)], text_rows, sems.at[0])
    fetch.start()
    shift = offset - begin
    pick = (iota((WINDOW, VQ), 0) - shift == iota((WINDOW, VQ), 1)).astype(f32).astype(bf16)
    half = row // 4
    wide = DL // 2
    embeds[:, pl.ds(pl.multiple_of(half * wide, 128), wide)] = jnp.dot(
        pick, mine[...], preferred_element_type=f32
    )
    embeds[:, pl.ds(pl.multiple_of((1 - half) * wide, 128), wide)] = jnp.dot(
        pick, other[...], preferred_element_type=f32
    )
    place = iota((WINDOW, DL), 0) - shift
    fetch.wait()
    rows = jnp.where((place >= 0) & (place < VQ), embeds[...], text_rows[...].astype(f32))
    done_rows[...] = norm_rows(rows, gain[...])
    store = pltpu.make_async_copy(done_rows, out.at[pl.ds(begin, WINDOW)], sems.at[1])
    store.start()
    store.wait()


def place(starts, mine, other, gain, text, normed):
    vmem = pl.BlockSpec(memory_space=pltpu.VMEM)
    anywhere = pl.BlockSpec(memory_space=pl.ANY)
    return pl.pallas_call(
        place_kernel,
        out_shape=jax.ShapeDtypeStruct(normed.shape, bf16),
        in_specs=[pl.BlockSpec(memory_space=pltpu.SMEM), vmem, vmem, vmem, anywhere, anywhere],
        out_specs=anywhere,
        input_output_aliases={5: 0},
        scratch_shapes=[
            pltpu.VMEM((WINDOW, DL), bf16),
            pltpu.VMEM((WINDOW, DL), f32),
            pltpu.VMEM((WINDOW, DL), bf16),
            pltpu.SemaphoreType.DMA((2,)),
        ],
        compiler_params=pltpu.CompilerParams(vmem_limit_bytes=24 * MIB),
        name="place",
    )(starts, mine, other, gain, text, normed)


def per_device(
    frame_feats, selected, counts, video_start, queries, frame_pos, w_query, w_key, w_value, w_out,
    ln_gain, ln_bias, proj_weight, proj_bias, text_embeds, norm_gain,
):
    def swap(x, mask):
        return lax.ppermute(x, "tm", [(k, k ^ mask) for k in range(8)])

    near = swap(proj_weight, 2)
    twin = swap(proj_weight, 1)
    parts = attend(
        selected, counts, video_start, frame_feats, frame_pos, queries, w_query, w_key, w_value
    )
    gain = norm_gain.reshape(1, DL)
    parts, text = lax.optimization_barrier((parts, text_embeds))
    received = lax.all_to_all(parts, "video", split_axis=0, concat_axis=0, tiled=True)
    normed = norm_text(text, gain)
    received, normed, near = lax.optimization_barrier((received, normed, near))
    rows = combine(received, queries, w_out, ln_gain, ln_bias)
    weights = (proj_weight, twin, near, swap(near, 1))
    bias = proj_bias.reshape(1, DL)
    other_rows = swap(rows, 6)
    mine = project(rows, weights, bias)
    other_rows, mine = lax.optimization_barrier((other_rows, mine))
    theirs = project(other_rows, weights, bias)
    other = swap(theirs, 6)
    return place(video_start, mine, other, gain, text_embeds, normed)


def solution(mesh):
    in_specs = (
        P("tm", "video", None, None), P("tm", None), P("tm"), P(), P(), P(), P(), P(), P(), P(),
        P(), P(), P(None, "tm"), P(), P(("tm", "video"), None), P(),
    )
    return jax.shard_map(
        per_device, mesh=mesh, in_specs=in_specs, out_specs=P(("tm", "video"), None), check_vma=False
    )
```

```python
import math

import jax
import jax.numpy as jnp
from jax import lax
from jax.experimental import pallas as pl
from jax.experimental.pallas import tpu as pltpu
from jax.sharding import PartitionSpec as P

HEADS = 12
HD = 64
WIDTH = HEADS * HD
VQ = 32
QF = 32
DL = 5120
SLOTS = 4
COLUMNS = 16
BLOCK = 256
SHARE = DL // 8
WINDOW = 48
STATS = 128
CHUNK = 8
NEAR = 6
MERGE_VMEM = 66_100_000
GROUP = 4
NEG = -1e30
MIB = 1 << 20

f32 = jnp.float32
bf16 = jnp.bfloat16


def iota(shape, axis):
    return lax.broadcasted_iota(jnp.int32, shape, axis)


def attend_kernel(
    selected_in, counts_in, starts_in, frames, pos_in, queries_in, w_query_in, w_key_in, w_value_in, out,
    selected, counts, starts, pos, queries, w_query, w_key, w_value, x_raw, x_keys, scores, values,
    folded, pos_wide, staged, scalar_sems, sems, weight_sems, out_sems,
):
    row = lax.axis_index("tm")
    column = lax.axis_index("video")
    scalars = [
        pltpu.make_async_copy(source, target, scalar_sems.at[i])
        for i, (source, target) in enumerate(
            ((selected_in, selected), (counts_in, counts), (starts_in, starts))
        )
    ]
    loads = [
        pltpu.make_async_copy(source, target, weight_sems.at[i])
        for i, (source, target) in enumerate((
            (queries_in, queries), (w_query_in, w_query), (w_key_in, w_key), (pos_in, pos),
            (w_value_in, w_value),
        ))
    ]
    for copy in scalars + loads:
        copy.start()
    for copy in scalars:
        copy.wait()

    def slot(video, j):
        count = counts[video]
        last = jnp.maximum(count >> 4, 1) - 1
        k = ((column * count) >> 4) + jnp.minimum(j, last)
        frame = selected[video, k] - column * 8
        live = (j <= last) & (frame >= 0) & (frame < 8)
        return k, jnp.clip(frame, 0, 7), live

    def fetch(video):
        for j in range(SLOTS):
            _, frame, _ = slot(video, j)
            pltpu.make_async_copy(
                frames.at[video, frame], x_raw.at[video * SLOTS + j], sems.at[video]
            ).start()

    pl.loop(0, COLUMNS)(fetch)
    for copy in loads[:2]:
        copy.wait()
    query = jnp.dot(queries[...], w_query[...], preferred_element_type=f32).astype(bf16)
    query = query * jnp.asarray(1.0 / math.sqrt(HD), bf16)
    loads[2].wait()
    for g in range(HEADS // GROUP):
        wide = GROUP * HD
        part = query[:, g * wide:(g + 1) * wide]
        part = jnp.concatenate([part] * GROUP, axis=0)
        same = iota(part.shape, 0) // VQ == iota(part.shape, 1) // HD
        part = jnp.where(same, part, jnp.zeros_like(part))
        fold = lax.dot_general(
            part, w_key[:, g * wide:(g + 1) * wide], (((1,), (1,)), ((), ())),
            preferred_element_type=f32,
        )
        rows = GROUP * VQ
        folded[g * rows:(g + 1) * rows, :] = fold.astype(bf16)
    loads[3].wait()
    pos_wide[...] = pos[...].astype(f32)

    lane = iota((VQ, STATS), 1)
    stat_head = lane % HEADS
    stat_part = lane // HEADS
    piece = stat_part % 3

    keys = SLOTS * QF

    def wait(chunk):
        for t in range(CHUNK):
            video = chunk * CHUNK + t
            pltpu.make_async_copy(
                frames.at[video, pl.ds(0, SLOTS)], x_raw.at[pl.ds(video * SLOTS, SLOTS)], sems.at[video]
            ).wait()

    def add(chunk, x_keys):
        for t in range(CHUNK):
            video = chunk * CHUNK + t
            for j in range(SLOTS):
                k, _, _ = slot(video, j)
                x = x_raw[video * SLOTS + j].astype(f32) + pos_wide[pl.ds(k, 1), :]
                at = (t * SLOTS + j) * QF
                x_keys[at:at + QF, :] = x.astype(bf16)

    def score(x_keys, scores, values):
        x = x_keys[...]
        scores[...] = lax.dot_general(folded[...], x, (((1,), (1,)), ((), ())), preferred_element_type=f32)
        values[...] = jnp.dot(x, w_value[...], preferred_element_type=f32).astype(bf16)

    def send(video):
        block = ((starts[row * COLUMNS + video] - row * (COLUMNS * BLOCK)) >> 8) & (COLUMNS - 1)
        return pltpu.make_async_copy(staged.at[video], out.at[block], out_sems.at[video])

    def finish(chunk, scores, values):
        for t in range(CHUNK):
            video = chunk * CHUNK + t
            alive = jnp.int32(0)
            for j in range(SLOTS):
                alive = alive + slot(video, j)[2].astype(jnp.int32)
            hidden = jnp.where(iota((1, keys), 1) < alive * QF, 0.0, NEG)
            s = scores[:, t * keys:(t + 1) * keys] + hidden
            top = jnp.max(s, axis=1, keepdims=True)
            p = jnp.exp(s - top)
            total = jnp.sum(p, axis=1, keepdims=True)
            p = p.astype(bf16)
            for g in range(HEADS // GROUP):
                wide = GROUP * HD
                rows = GROUP * VQ
                full = jnp.dot(
                    p[g * rows:(g + 1) * rows], values[t * keys:(t + 1) * keys, g * wide:(g + 1) * wide],
                    preferred_element_type=f32,
                )
                head = iota((VQ, wide), 1) // HD
                context = full[:VQ]
                for h in range(1, GROUP):
                    context = jnp.where(head == h, full[h * VQ:(h + 1) * VQ], context)
                staged[video, :, g * wide:(g + 1) * wide] = context.astype(bf16)
            stat = jnp.zeros((VQ, STATS), f32)
            for h in range(HEADS):
                one = jnp.where(stat_part < 3, top[h * VQ:(h + 1) * VQ], total[h * VQ:(h + 1) * VQ])
                stat = jnp.where(stat_head == h, one, stat)
            high = stat.astype(bf16).astype(f32)
            mid = (stat - high).astype(bf16).astype(f32)
            low = stat - high - mid
            stat = jnp.where(piece == 0, high, jnp.where(piece == 1, mid, low))
            stat = jnp.where(stat_part < 6, stat, 0.0)
            staged[video, :, WIDTH:] = stat.astype(bf16)

    chunks = COLUMNS // CHUNK
    wait(0)
    add(0, x_keys.at[0])
    loads[4].wait()
    for chunk in range(chunks + 1):
        if chunk + 1 < chunks:
            wait(chunk + 1)
        if chunk < chunks:
            score(x_keys.at[chunk % 2], scores.at[chunk % 2], values.at[chunk % 2])
        if chunk + 1 < chunks:
            add(chunk + 1, x_keys.at[(chunk + 1) % 2])
        if chunk > 0:
            finish(chunk - 1, scores.at[(chunk - 1) % 2], values.at[(chunk - 1) % 2])
        if chunk > 0:
            for t in range(CHUNK):
                send((chunk - 1) * CHUNK + t).start()
    for video in range(COLUMNS):
        send(video).wait()


def attend(selected, counts, starts, frames, pos, queries, w_query, w_key, w_value):
    return pl.pallas_call(
        attend_kernel,
        out_shape=jax.ShapeDtypeStruct((COLUMNS, VQ, WIDTH + STATS), bf16),
        in_specs=[pl.BlockSpec(memory_space=pl.ANY)] * 9,
        out_specs=pl.BlockSpec(memory_space=pl.ANY),
        scratch_shapes=[
            pltpu.SMEM(selected.shape, jnp.int32),
            pltpu.SMEM(counts.shape, jnp.int32),
            pltpu.SMEM(starts.shape, jnp.int32),
            pltpu.VMEM(pos.shape, bf16),
            pltpu.VMEM(queries.shape, bf16),
            pltpu.VMEM((WIDTH, WIDTH), bf16),
            pltpu.VMEM((WIDTH, WIDTH), bf16),
            pltpu.VMEM((WIDTH, WIDTH), bf16),
            pltpu.VMEM((COLUMNS * SLOTS, QF, WIDTH), bf16),
            pltpu.VMEM((2, CHUNK * SLOTS * QF, WIDTH), bf16),
            pltpu.VMEM((2, HEADS * VQ, CHUNK * SLOTS * QF), f32),
            pltpu.VMEM((2, CHUNK * SLOTS * QF, WIDTH), bf16),
            pltpu.VMEM((HEADS * VQ, WIDTH), bf16),
            pltpu.VMEM(pos.shape, f32),
            pltpu.VMEM((COLUMNS, VQ, WIDTH + STATS), bf16),
            pltpu.SemaphoreType.DMA((3,)),
            pltpu.SemaphoreType.DMA((COLUMNS,)),
            pltpu.SemaphoreType.DMA((5,)),
            pltpu.SemaphoreType.DMA((COLUMNS,)),
        ],
        compiler_params=pltpu.CompilerParams(vmem_limit_bytes=60 * MIB),
        cost_estimate=pl.CostEstimate(
            flops=9_000_000_000, bytes_accessed=8_000_000, transcendentals=800_000
        ),
        name="attend",
    )(selected, counts, starts, frames, pos, queries, w_query, w_key, w_value)


def nearer(device):
    return device ^ (2 + 4 * (device & 1))


def crossing(device):
    return device ^ (7 - 4 * (device & 1))


def blocks_of(device):
    twin = device ^ 1
    return (
        device, twin, nearer(device) ^ 1, nearer(twin) ^ 1, nearer(device), device ^ 4, nearer(twin), device ^ 5
    )


def window_of(starts):
    row = lax.axis_index("tm")
    column = lax.axis_index("video")
    first = (row * COLUMNS + column) * BLOCK
    offset = jnp.int32(0)
    for w in range(COLUMNS):
        at = starts[row * COLUMNS + w] - first
        offset = offset + jnp.where((at >= 0) & (at < BLOCK), at, 0)
    begin = pl.multiple_of(jnp.minimum(offset >> 4, (BLOCK - WINDOW) // 16) * 16, 16)
    return begin, offset - begin


def merge_kernel(
    parts_in, queries_in, w_out_in, gain_in, bias_in, starts_in, proj_bias_in, text, w0, w1, w2, w3, w4, w5,
    rows_out, wide_out, rest_out,
    parts, queries, w_out, gain, bias, starts, proj_bias, weights, window, sems, weight_sems,
):
    loads = [
        pltpu.make_async_copy(source, target, sems.at[i])
        for i, (source, target) in enumerate((
            (starts_in, starts), (parts_in, parts), (w_out_in, w_out), (queries_in, queries), (gain_in, gain),
            (bias_in, bias), (proj_bias_in, proj_bias),
        ))
    ]
    blocks = [
        pltpu.make_async_copy(source, weights.at[i], weight_sems.at[i])
        for i, source in enumerate((w0, w1, w2, w3, w4, w5))
    ]
    for copy in loads + blocks:
        copy.start()
    loads[0].wait()
    begin, shift = window_of(starts)
    fetch = pltpu.make_async_copy(text.at[pl.ds(begin, WINDOW)], window, sems.at[7])
    fetch.start()
    loads[1].wait()
    stat = parts[:, :, WIDTH:].astype(f32).reshape(COLUMNS * VQ, STATS)

    def shifted(n):
        return pltpu.roll(stat, STATS - n * HEADS, 1)

    tops = stat + shifted(1) + shifted(2)
    totals = shifted(3) + shifted(4) + shifted(5)
    lane = iota((VQ, STATS), 1)
    real = lane < HEADS
    tops = [jnp.where(real, tops[c * VQ:(c + 1) * VQ], 0.0) for c in range(COLUMNS)]
    totals = [jnp.where(real, totals[c * VQ:(c + 1) * VQ], 1.0) for c in range(COLUMNS)]
    top = tops[0]
    for c in range(1, COLUMNS):
        top = jnp.maximum(top, tops[c])
    scales = [jnp.exp(t - top) for t in tops]
    total = scales[0] * totals[0]
    for c in range(1, COLUMNS):
        total = total + scales[c] * totals[c]
    inverse = jnp.where(real, 1.0 / total, 0.0)
    weight = jnp.concatenate([s * inverse for s in scales], axis=0)
    high = weight.astype(bf16)
    low = (weight - high.astype(f32)).astype(bf16)
    spread = (iota((2 * STATS, WIDTH), 0) % STATS == iota((2 * STATS, WIDTH), 1) // HD).astype(f32).astype(bf16)
    weight = jnp.dot(jnp.concatenate([high, low], axis=1), spread, preferred_element_type=f32)
    context = jnp.zeros((VQ, WIDTH), f32)
    for c in range(COLUMNS):
        context = context + weight[c * VQ:(c + 1) * VQ] * parts[c, :, :WIDTH].astype(f32)
    for copy in loads[2:]:
        copy.wait()
    residual = jnp.dot(context.astype(bf16), w_out[...], preferred_element_type=f32) + queries[...].astype(f32)
    mean = jnp.mean(residual, axis=-1, keepdims=True)
    centred = residual - mean
    variance = jnp.mean(centred * centred, axis=-1, keepdims=True)
    rows = (centred * lax.rsqrt(variance + 1e-12) * gain[...] + bias[...]).astype(bf16)
    pick = (iota((WINDOW, VQ), 0) - shift == iota((WINDOW, VQ), 1)).astype(f32).astype(bf16)
    rows = jnp.dot(pick, rows, preferred_element_type=f32).astype(bf16)
    rows_out[...] = rows
    place = iota((WINDOW, SHARE), 0) - shift
    inside = (place >= 0) & (place < VQ)
    fetch.wait()
    for i, block in enumerate(blocks_of(lax.axis_index("tm"))):
        here = pl.ds(pl.multiple_of(block * SHARE, 128), SHARE)
        text_rows = window[:, here]
        if i < NEAR:
            blocks[i].wait()
            result = jnp.dot(rows, weights[i], preferred_element_type=f32) + proj_bias[:, here]
            wide_out[:, i * SHARE:(i + 1) * SHARE] = jnp.where(
                inside, result, text_rows.astype(f32)
            ).astype(bf16)
        else:
            rest_out[:, (i - NEAR) * SHARE:(i - NEAR + 1) * SHARE] = text_rows


def merge(parts, queries, w_out, gain, bias, starts, proj_bias, text, weights):
    vmem = pl.BlockSpec(memory_space=pltpu.VMEM)
    anywhere = pl.BlockSpec(memory_space=pl.ANY)
    return pl.pallas_call(
        merge_kernel,
        out_shape=[
            jax.ShapeDtypeStruct((WINDOW, WIDTH), bf16),
            jax.ShapeDtypeStruct((WINDOW, NEAR * SHARE), bf16),
            jax.ShapeDtypeStruct((WINDOW, DL - NEAR * SHARE), bf16),
        ],
        in_specs=[anywhere] * 14,
        out_specs=[vmem, vmem, vmem],
        scratch_shapes=[
            pltpu.VMEM(parts.shape, bf16),
            pltpu.VMEM(queries.shape, bf16),
            pltpu.VMEM((WIDTH, WIDTH), bf16),
            pltpu.VMEM((1, WIDTH), f32),
            pltpu.VMEM((1, WIDTH), f32),
            pltpu.SMEM(starts.shape, jnp.int32),
            pltpu.VMEM((1, DL), f32),
            pltpu.VMEM((NEAR, WIDTH, SHARE), bf16),
            pltpu.VMEM((WINDOW, DL), bf16),
            pltpu.SemaphoreType.DMA((8,)),
            pltpu.SemaphoreType.DMA((NEAR,)),
        ],
        compiler_params=pltpu.CompilerParams(vmem_limit_bytes=MERGE_VMEM),
        cost_estimate=pl.CostEstimate(flops=500_000_000, bytes_accessed=9_000_000, transcendentals=70_000),
        name="merge",
    )(parts, queries, w_out, gain, bias, starts, proj_bias, text, *weights)


def place_kernel(
    rows_in, wide_in, rest_in, starts_in, proj_bias_in, norm_gain_in, normed, w6, w7, done,
    starts, proj_bias, norm_gain, weights, wide, done_rows, sems, weight_sems,
):
    loads = [
        pltpu.make_async_copy(source, target, sems.at[i])
        for i, (source, target) in enumerate((
            (starts_in, starts), (proj_bias_in, proj_bias), (norm_gain_in, norm_gain),
        ))
    ]
    blocks = [
        pltpu.make_async_copy(source, weights.at[i], weight_sems.at[i]) for i, source in enumerate((w6, w7))
    ]
    for copy in loads + blocks:
        copy.start()
    rows = rows_in[...]
    squares = jnp.zeros((WINDOW, 1), f32)
    all_blocks = blocks_of(lax.axis_index("tm"))
    for i, block in enumerate(all_blocks):
        here = pl.ds(pl.multiple_of(block * SHARE, 128), SHARE)
        if i < NEAR:
            embeds = wide_in[:, i * SHARE:(i + 1) * SHARE].astype(f32)
        else:
            if i == NEAR:
                loads[0].wait()
                begin, shift = window_of(starts)
                place = iota((WINDOW, SHARE), 0) - shift
                inside = (place >= 0) & (place < VQ)
                loads[1].wait()
            blocks[i - NEAR].wait()
            result = jnp.dot(rows, weights[i - NEAR], preferred_element_type=f32) + proj_bias[:, here]
            text_rows = rest_in[:, (i - NEAR) * SHARE:(i - NEAR + 1) * SHARE]
            embeds = jnp.where(inside, result, text_rows.astype(f32)).astype(bf16).astype(f32)
        wide[:, i * SHARE:(i + 1) * SHARE] = embeds
        squares = squares + jnp.sum(embeds * embeds, axis=-1, keepdims=True)
    scale = lax.rsqrt(squares * (1.0 / DL) + 1e-05)
    loads[2].wait()
    for i, block in enumerate(all_blocks):
        here = pl.ds(pl.multiple_of(block * SHARE, 128), SHARE)
        done_rows[:, here] = (wide[:, i * SHARE:(i + 1) * SHARE] * scale * norm_gain[:, here]).astype(bf16)
    store = pltpu.make_async_copy(done_rows, done.at[pl.ds(begin, WINDOW)], sems.at[3])
    store.start()
    store.wait()


def place(rows, wide, rest, starts, proj_bias, norm_gain, normed, weights):
    vmem = pl.BlockSpec(memory_space=pltpu.VMEM)
    anywhere = pl.BlockSpec(memory_space=pl.ANY)
    return pl.pallas_call(
        place_kernel,
        out_shape=jax.ShapeDtypeStruct(normed.shape, bf16),
        in_specs=[vmem] * 3 + [anywhere] * 6,
        out_specs=anywhere,
        input_output_aliases={6: 0},
        scratch_shapes=[
            pltpu.SMEM(starts.shape, jnp.int32),
            pltpu.VMEM((1, DL), f32),
            pltpu.VMEM((1, DL), f32),
            pltpu.VMEM((8 - NEAR, WIDTH, SHARE), bf16),
            pltpu.VMEM((WINDOW, DL), f32),
            pltpu.VMEM((WINDOW, DL), bf16),
            pltpu.SemaphoreType.DMA((4,)),
            pltpu.SemaphoreType.DMA((8 - NEAR,)),
        ],
        compiler_params=pltpu.CompilerParams(vmem_limit_bytes=MERGE_VMEM),
        name="place",
    )(rows, wide, rest, starts, proj_bias, norm_gain, normed, *weights)


def norm_rows(wide, gain):
    squares = jnp.mean(wide * wide, axis=-1, keepdims=True)
    return (wide * lax.rsqrt(squares + 1e-05) * gain).astype(bf16)


def text_kernel(text, gain, out):
    out[...] = norm_rows(text[...].astype(f32), gain[...])


def norm_text(text, gain):
    rows = 64
    return pl.pallas_call(
        text_kernel,
        out_shape=jax.ShapeDtypeStruct(text.shape, bf16),
        grid=(text.shape[0] // rows,),
        in_specs=[
            pl.BlockSpec((rows, DL), lambda i: (i, 0)),
            pl.BlockSpec((1, DL), lambda i: (0, 0)),
        ],
        out_specs=pl.BlockSpec((rows, DL), lambda i: (i, 0)),
        compiler_params=pltpu.CompilerParams(vmem_limit_bytes=24 * MIB),
        cost_estimate=pl.CostEstimate(flops=8_000_000, bytes_accessed=5_300_000, transcendentals=256),
        name="norm_text",
    )(text, gain)


def per_device(
    frame_feats, selected, counts, video_start, queries, frame_pos, w_query, w_key, w_value, w_out,
    ln_gain, ln_bias, proj_weight, proj_bias, text_embeds, norm_gain,
):
    def move(x, target):
        return lax.ppermute(x, "tm", [(k, target(k)) for k in range(8)])

    def twin_of(device):
        return device ^ 1

    near_twin = move(proj_weight, crossing)
    twin = move(proj_weight, twin_of)
    parts = attend(
        selected, counts, video_start, frame_feats, frame_pos, queries, w_query, w_key, w_value
    )
    gain = norm_gain.reshape(1, DL)
    bias = proj_bias.reshape(1, DL)
    parts, text, share = lax.optimization_barrier((parts, text_embeds, proj_weight))
    far = move(near_twin, crossing)
    near = move(share, nearer)
    received = lax.all_to_all(parts, "video", split_axis=0, concat_axis=0, tiled=True)
    normed = norm_text(text, gain)
    ln_gain, ln_bias = ln_gain.reshape(1, WIDTH), ln_bias.reshape(1, WIDTH)
    received, normed, near, far, ln_gain, ln_bias, bias = lax.optimization_barrier(
        (received, normed, near, far, ln_gain, ln_bias, bias)
    )
    other_near_twin = move(near_twin, twin_of)
    other_near, far_twin = move(near, twin_of), move(far, twin_of)
    rows, wide, rest = merge(
        received, queries, w_out, ln_gain, ln_bias, video_start, bias, text_embeds,
        (proj_weight, twin, near_twin, other_near_twin, near, far),
    )
    rows, wide, rest, other_near, far_twin = lax.optimization_barrier((rows, wide, rest, other_near, far_twin))
    return place(rows, wide, rest, video_start, bias, gain, normed, (other_near, far_twin))


def solution(mesh):
    in_specs = (
        P("tm", "video", None, None), P("tm", None), P("tm"), P(), P(), P(), P(), P(), P(), P(),
        P(), P(), P(None, "tm"), P(), P(("tm", "video"), None), P(),
    )
    return jax.shard_map(
        per_device, mesh=mesh, in_specs=in_specs, out_specs=P(("tm", "video"), None), check_vma=False
    )
```

```python
import math

import jax
import jax.numpy as jnp
from jax import lax
from jax.experimental import pallas as pl
from jax.experimental.pallas import tpu as pltpu
from jax.sharding import PartitionSpec as P

HEADS = 12
HD = 64
WIDTH = HEADS * HD
VQ = 32
QF = 32
DL = 5120
SLOTS = 4
COLUMNS = 16
BLOCK = 256
SHARE = DL // 8
WINDOW = 48
STATS = 128
CHUNK = 8
NEAR = 6
MERGE_VMEM = 66_100_000
GROUP = 4
NEG = -1e30
MIB = 1 << 20

f32 = jnp.float32
bf16 = jnp.bfloat16


def iota(shape, axis):
    return lax.broadcasted_iota(jnp.int32, shape, axis)


def attend_kernel(
    selected_in, counts_in, starts_in, frames, pos_in, queries_in, w_query_in, w_key_in, w_value_in, out,
    selected, counts, starts, pos, queries, w_query, w_key, w_value, x_raw, x_keys, scores, values,
    folded, pos_wide, staged, scalar_sems, sems, weight_sems, out_sems,
):
    row = lax.axis_index("tm")
    column = lax.axis_index("video")
    scalars = [
        pltpu.make_async_copy(source, target, scalar_sems.at[i])
        for i, (source, target) in enumerate(
            ((selected_in, selected), (counts_in, counts), (starts_in, starts))
        )
    ]
    loads = [
        pltpu.make_async_copy(source, target, weight_sems.at[i])
        for i, (source, target) in enumerate((
            (queries_in, queries), (w_query_in, w_query), (w_key_in, w_key), (pos_in, pos),
            (w_value_in, w_value),
        ))
    ]
    for copy in scalars + loads:
        copy.start()
    for copy in scalars:
        copy.wait()

    def slot(video, j):
        count = counts[video]
        last = jnp.maximum(count >> 4, 1) - 1
        k = ((column * count) >> 4) + jnp.minimum(j, last)
        frame = selected[video, k] - column * 8
        live = (j <= last) & (frame >= 0) & (frame < 8)
        return k, jnp.clip(frame, 0, 7), live

    def fetch(video):
        for j in range(SLOTS):
            _, frame, _ = slot(video, j)
            pltpu.make_async_copy(
                frames.at[video, frame], x_raw.at[video * SLOTS + j], sems.at[video]
            ).start()

    pl.loop(0, COLUMNS)(fetch)
    for copy in loads[:2]:
        copy.wait()
    query = jnp.dot(queries[...], w_query[...], preferred_element_type=f32).astype(bf16)
    query = query * jnp.asarray(1.0 / math.sqrt(HD), bf16)
    loads[2].wait()
    for g in range(HEADS // GROUP):
        wide = GROUP * HD
        part = query[:, g * wide:(g + 1) * wide]
        part = jnp.concatenate([part] * GROUP, axis=0)
        same = iota(part.shape, 0) // VQ == iota(part.shape, 1) // HD
        part = jnp.where(same, part, jnp.zeros_like(part))
        fold = lax.dot_general(
            part, w_key[:, g * wide:(g + 1) * wide], (((1,), (1,)), ((), ())),
            preferred_element_type=f32,
        )
        rows = GROUP * VQ
        folded[g * rows:(g + 1) * rows, :] = fold.astype(bf16)
    loads[3].wait()
    pos_wide[...] = pos[...].astype(f32)

    lane = iota((VQ, STATS), 1)
    stat_head = lane % HEADS
    stat_part = lane // HEADS
    piece = stat_part % 3

    keys = SLOTS * QF

    def wait(chunk):
        for t in range(CHUNK):
            video = chunk * CHUNK + t
            pltpu.make_async_copy(
                frames.at[video, pl.ds(0, SLOTS)], x_raw.at[pl.ds(video * SLOTS, SLOTS)], sems.at[video]
            ).wait()

    def add(chunk, x_keys):
        for t in range(CHUNK):
            video = chunk * CHUNK + t
            for j in range(SLOTS):
                k, _, _ = slot(video, j)
                x = x_raw[video * SLOTS + j].astype(f32) + pos_wide[pl.ds(k, 1), :]
                at = (t * SLOTS + j) * QF
                x_keys[at:at + QF, :] = x.astype(bf16)

    def score(x_keys, scores, values):
        x = x_keys[...]
        scores[...] = lax.dot_general(folded[...], x, (((1,), (1,)), ((), ())), preferred_element_type=f32)
        values[...] = jnp.dot(x, w_value[...], preferred_element_type=f32).astype(bf16)

    def send(video):
        block = ((starts[row * COLUMNS + video] - row * (COLUMNS * BLOCK)) >> 8) & (COLUMNS - 1)
        return pltpu.make_async_copy(staged.at[video], out.at[block], out_sems.at[video])

    def finish(chunk, scores, values):
        for t in range(CHUNK):
            video = chunk * CHUNK + t
            alive = jnp.int32(0)
            for j in range(SLOTS):
                alive = alive + slot(video, j)[2].astype(jnp.int32)
            hidden = jnp.where(iota((1, keys), 1) < alive * QF, 0.0, NEG)
            s = scores[:, t * keys:(t + 1) * keys] + hidden
            top = jnp.max(s, axis=1, keepdims=True)
            p = jnp.exp(s - top)
            total = jnp.sum(p, axis=1, keepdims=True)
            p = p.astype(bf16)
            for g in range(HEADS // GROUP):
                wide = GROUP * HD
                rows = GROUP * VQ
                full = jnp.dot(
                    p[g * rows:(g + 1) * rows], values[t * keys:(t + 1) * keys, g * wide:(g + 1) * wide],
                    preferred_element_type=f32,
                )
                head = iota((VQ, wide), 1) // HD
                context = full[:VQ]
                for h in range(1, GROUP):
                    context = jnp.where(head == h, full[h * VQ:(h + 1) * VQ], context)
                staged[video, :, g * wide:(g + 1) * wide] = context.astype(bf16)
            stat = jnp.zeros((VQ, STATS), f32)
            for h in range(HEADS):
                one = jnp.where(stat_part < 3, top[h * VQ:(h + 1) * VQ], total[h * VQ:(h + 1) * VQ])
                stat = jnp.where(stat_head == h, one, stat)
            high = stat.astype(bf16).astype(f32)
            mid = (stat - high).astype(bf16).astype(f32)
            low = stat - high - mid
            stat = jnp.where(piece == 0, high, jnp.where(piece == 1, mid, low))
            stat = jnp.where(stat_part < 6, stat, 0.0)
            staged[video, :, WIDTH:] = stat.astype(bf16)

    chunks = COLUMNS // CHUNK
    wait(0)
    add(0, x_keys.at[0])
    loads[4].wait()
    for chunk in range(chunks + 1):
        if chunk + 1 < chunks:
            wait(chunk + 1)
        if chunk < chunks:
            score(x_keys.at[chunk % 2], scores.at[chunk % 2], values.at[chunk % 2])
        if chunk + 1 < chunks:
            add(chunk + 1, x_keys.at[(chunk + 1) % 2])
        if chunk > 0:
            finish(chunk - 1, scores.at[(chunk - 1) % 2], values.at[(chunk - 1) % 2])
        if chunk > 0:
            for t in range(CHUNK):
                send((chunk - 1) * CHUNK + t).start()
    for video in range(COLUMNS):
        send(video).wait()


def attend(selected, counts, starts, frames, pos, queries, w_query, w_key, w_value):
    return pl.pallas_call(
        attend_kernel,
        out_shape=jax.ShapeDtypeStruct((COLUMNS, VQ, WIDTH + STATS), bf16),
        in_specs=[pl.BlockSpec(memory_space=pl.ANY)] * 9,
        out_specs=pl.BlockSpec(memory_space=pl.ANY),
        scratch_shapes=[
            pltpu.SMEM(selected.shape, jnp.int32),
            pltpu.SMEM(counts.shape, jnp.int32),
            pltpu.SMEM(starts.shape, jnp.int32),
            pltpu.VMEM(pos.shape, bf16),
            pltpu.VMEM(queries.shape, bf16),
            pltpu.VMEM((WIDTH, WIDTH), bf16),
            pltpu.VMEM((WIDTH, WIDTH), bf16),
            pltpu.VMEM((WIDTH, WIDTH), bf16),
            pltpu.VMEM((COLUMNS * SLOTS, QF, WIDTH), bf16),
            pltpu.VMEM((2, CHUNK * SLOTS * QF, WIDTH), bf16),
            pltpu.VMEM((2, HEADS * VQ, CHUNK * SLOTS * QF), f32),
            pltpu.VMEM((2, CHUNK * SLOTS * QF, WIDTH), bf16),
            pltpu.VMEM((HEADS * VQ, WIDTH), bf16),
            pltpu.VMEM(pos.shape, f32),
            pltpu.VMEM((COLUMNS, VQ, WIDTH + STATS), bf16),
            pltpu.SemaphoreType.DMA((3,)),
            pltpu.SemaphoreType.DMA((COLUMNS,)),
            pltpu.SemaphoreType.DMA((5,)),
            pltpu.SemaphoreType.DMA((COLUMNS,)),
        ],
        compiler_params=pltpu.CompilerParams(vmem_limit_bytes=60 * MIB),
        cost_estimate=pl.CostEstimate(
            flops=9_000_000_000, bytes_accessed=8_000_000, transcendentals=800_000
        ),
        name="attend",
    )(selected, counts, starts, frames, pos, queries, w_query, w_key, w_value)


def nearer(device):
    return device ^ (2 + 4 * (device & 1))


def crossing(device):
    return device ^ (7 - 4 * (device & 1))


def blocks_of(device):
    twin = device ^ 1
    return (
        device, twin, nearer(device) ^ 1, nearer(twin) ^ 1, nearer(device), device ^ 4, nearer(twin), device ^ 5
    )


def window_of(starts):
    row = lax.axis_index("tm")
    column = lax.axis_index("video")
    first = (row * COLUMNS + column) * BLOCK
    offset = jnp.int32(0)
    for w in range(COLUMNS):
        at = starts[row * COLUMNS + w] - first
        offset = offset + jnp.where((at >= 0) & (at < BLOCK), at, 0)
    begin = pl.multiple_of(jnp.minimum(offset >> 4, (BLOCK - WINDOW) // 16) * 16, 16)
    return begin, offset - begin


def merge_kernel(
    parts_in, queries_in, w_out_in, gain_in, bias_in, starts_in, proj_bias_in, text, w0, w1, w2, w3, w4, w5,
    rows_out, wide_out, rest_out,
    parts, queries, w_out, gain, bias, starts, proj_bias, weights, window, sems, weight_sems,
):
    loads = [
        pltpu.make_async_copy(source, target, sems.at[i])
        for i, (source, target) in enumerate((
            (starts_in, starts), (parts_in, parts), (w_out_in, w_out), (queries_in, queries), (gain_in, gain),
            (bias_in, bias), (proj_bias_in, proj_bias),
        ))
    ]
    blocks = [
        pltpu.make_async_copy(source, weights.at[i], weight_sems.at[i])
        for i, source in enumerate((w0, w1, w2, w3, w4, w5))
    ]
    for copy in loads:
        copy.start()
    loads[0].wait()
    begin, shift = window_of(starts)
    fetch = pltpu.make_async_copy(text.at[pl.ds(begin, WINDOW)], window, sems.at[7])
    fetch.start()
    loads[1].wait()
    for copy in blocks:
        copy.start()
    stat = parts[:, :, WIDTH:].astype(f32).reshape(COLUMNS * VQ, STATS)

    def shifted(n):
        return pltpu.roll(stat, STATS - n * HEADS, 1)

    tops = stat + shifted(1) + shifted(2)
    totals = shifted(3) + shifted(4) + shifted(5)
    lane = iota((VQ, STATS), 1)
    real = lane < HEADS
    tops = [jnp.where(real, tops[c * VQ:(c + 1) * VQ], 0.0) for c in range(COLUMNS)]
    totals = [jnp.where(real, totals[c * VQ:(c + 1) * VQ], 1.0) for c in range(COLUMNS)]
    top = tops[0]
    for c in range(1, COLUMNS):
        top = jnp.maximum(top, tops[c])
    scales = [jnp.exp(t - top) for t in tops]
    total = scales[0] * totals[0]
    for c in range(1, COLUMNS):
        total = total + scales[c] * totals[c]
    inverse = jnp.where(real, 1.0 / total, 0.0)
    weight = jnp.concatenate([s * inverse for s in scales], axis=0)
    high = weight.astype(bf16)
    low = (weight - high.astype(f32)).astype(bf16)
    spread = (iota((2 * STATS, WIDTH), 0) % STATS == iota((2 * STATS, WIDTH), 1) // HD).astype(f32).astype(bf16)
    weight = jnp.dot(jnp.concatenate([high, low], axis=1), spread, preferred_element_type=f32)
    context = jnp.zeros((VQ, WIDTH), f32)
    for c in range(COLUMNS):
        context = context + weight[c * VQ:(c + 1) * VQ] * parts[c, :, :WIDTH].astype(f32)
    for copy in loads[2:]:
        copy.wait()
    residual = jnp.dot(context.astype(bf16), w_out[...], preferred_element_type=f32) + queries[...].astype(f32)
    mean = jnp.mean(residual, axis=-1, keepdims=True)
    centred = residual - mean
    variance = jnp.mean(centred * centred, axis=-1, keepdims=True)
    rows = (centred * lax.rsqrt(variance + 1e-12) * gain[...] + bias[...]).astype(bf16)
    pick = (iota((WINDOW, VQ), 0) - shift == iota((WINDOW, VQ), 1)).astype(f32).astype(bf16)
    rows = jnp.dot(pick, rows, preferred_element_type=f32).astype(bf16)
    rows_out[...] = rows
    place = iota((WINDOW, SHARE), 0) - shift
    inside = (place >= 0) & (place < VQ)
    fetch.wait()
    for i, block in enumerate(blocks_of(lax.axis_index("tm"))):
        here = pl.ds(pl.multiple_of(block * SHARE, 128), SHARE)
        text_rows = window[:, here]
        if i < NEAR:
            blocks[i].wait()
            result = jnp.dot(rows, weights[i], preferred_element_type=f32) + proj_bias[:, here]
            wide_out[:, i * SHARE:(i + 1) * SHARE] = jnp.where(
                inside, result, text_rows.astype(f32)
            ).astype(bf16)
        else:
            rest_out[:, (i - NEAR) * SHARE:(i - NEAR + 1) * SHARE] = text_rows


def merge(parts, queries, w_out, gain, bias, starts, proj_bias, text, weights):
    vmem = pl.BlockSpec(memory_space=pltpu.VMEM)
    anywhere = pl.BlockSpec(memory_space=pl.ANY)
    return pl.pallas_call(
        merge_kernel,
        out_shape=[
            jax.ShapeDtypeStruct((WINDOW, WIDTH), bf16),
            jax.ShapeDtypeStruct((WINDOW, NEAR * SHARE), bf16),
            jax.ShapeDtypeStruct((WINDOW, DL - NEAR * SHARE), bf16),
        ],
        in_specs=[anywhere] * 14,
        out_specs=[vmem, vmem, vmem],
        scratch_shapes=[
            pltpu.VMEM(parts.shape, bf16),
            pltpu.VMEM(queries.shape, bf16),
            pltpu.VMEM((WIDTH, WIDTH), bf16),
            pltpu.VMEM((1, WIDTH), f32),
            pltpu.VMEM((1, WIDTH), f32),
            pltpu.SMEM(starts.shape, jnp.int32),
            pltpu.VMEM((1, DL), f32),
            pltpu.VMEM((NEAR, WIDTH, SHARE), bf16),
            pltpu.VMEM((WINDOW, DL), bf16),
            pltpu.SemaphoreType.DMA((8,)),
            pltpu.SemaphoreType.DMA((NEAR,)),
        ],
        compiler_params=pltpu.CompilerParams(vmem_limit_bytes=MERGE_VMEM),
        cost_estimate=pl.CostEstimate(flops=500_000_000, bytes_accessed=9_000_000, transcendentals=70_000),
        name="merge",
    )(parts, queries, w_out, gain, bias, starts, proj_bias, text, *weights)


def place_kernel(
    rows_in, wide_in, rest_in, starts_in, proj_bias_in, norm_gain_in, normed, w6, w7, done,
    starts, proj_bias, norm_gain, weights, wide, done_rows, sems, weight_sems,
):
    loads = [
        pltpu.make_async_copy(source, target, sems.at[i])
        for i, (source, target) in enumerate((
            (starts_in, starts), (proj_bias_in, proj_bias), (norm_gain_in, norm_gain),
        ))
    ]
    blocks = [
        pltpu.make_async_copy(source, weights.at[i], weight_sems.at[i]) for i, source in enumerate((w6, w7))
    ]
    for copy in loads + blocks:
        copy.start()
    rows = rows_in[...]
    squares = jnp.zeros((WINDOW, 1), f32)
    all_blocks = blocks_of(lax.axis_index("tm"))
    for i, block in enumerate(all_blocks):
        here = pl.ds(pl.multiple_of(block * SHARE, 128), SHARE)
        if i < NEAR:
            embeds = wide_in[:, i * SHARE:(i + 1) * SHARE].astype(f32)
        else:
            if i == NEAR:
                loads[0].wait()
                begin, shift = window_of(starts)
                place = iota((WINDOW, SHARE), 0) - shift
                inside = (place >= 0) & (place < VQ)
                loads[1].wait()
            blocks[i - NEAR].wait()
            result = jnp.dot(rows, weights[i - NEAR], preferred_element_type=f32) + proj_bias[:, here]
            text_rows = rest_in[:, (i - NEAR) * SHARE:(i - NEAR + 1) * SHARE]
            embeds = jnp.where(inside, result, text_rows.astype(f32)).astype(bf16).astype(f32)
        wide[:, i * SHARE:(i + 1) * SHARE] = embeds
        squares = squares + jnp.sum(embeds * embeds, axis=-1, keepdims=True)
    scale = lax.rsqrt(squares * (1.0 / DL) + 1e-05)
    loads[2].wait()
    for i, block in enumerate(all_blocks):
        here = pl.ds(pl.multiple_of(block * SHARE, 128), SHARE)
        done_rows[:, here] = (wide[:, i * SHARE:(i + 1) * SHARE] * scale * norm_gain[:, here]).astype(bf16)
    store = pltpu.make_async_copy(done_rows, done.at[pl.ds(begin, WINDOW)], sems.at[3])
    store.start()
    store.wait()


def place(rows, wide, rest, starts, proj_bias, norm_gain, normed, weights):
    vmem = pl.BlockSpec(memory_space=pltpu.VMEM)
    anywhere = pl.BlockSpec(memory_space=pl.ANY)
    return pl.pallas_call(
        place_kernel,
        out_shape=jax.ShapeDtypeStruct(normed.shape, bf16),
        in_specs=[vmem] * 3 + [anywhere] * 6,
        out_specs=anywhere,
        input_output_aliases={6: 0},
        scratch_shapes=[
            pltpu.SMEM(starts.shape, jnp.int32),
            pltpu.VMEM((1, DL), f32),
            pltpu.VMEM((1, DL), f32),
            pltpu.VMEM((8 - NEAR, WIDTH, SHARE), bf16),
            pltpu.VMEM((WINDOW, DL), f32),
            pltpu.VMEM((WINDOW, DL), bf16),
            pltpu.SemaphoreType.DMA((4,)),
            pltpu.SemaphoreType.DMA((8 - NEAR,)),
        ],
        compiler_params=pltpu.CompilerParams(vmem_limit_bytes=MERGE_VMEM),
        name="place",
    )(rows, wide, rest, starts, proj_bias, norm_gain, normed, *weights)


def norm_rows(wide, gain):
    squares = jnp.mean(wide * wide, axis=-1, keepdims=True)
    return (wide * lax.rsqrt(squares + 1e-05) * gain).astype(bf16)


def text_kernel(text, gain, out):
    out[...] = norm_rows(text[...].astype(f32), gain[...])


def norm_text(text, gain):
    rows = 64
    return pl.pallas_call(
        text_kernel,
        out_shape=jax.ShapeDtypeStruct(text.shape, bf16),
        grid=(text.shape[0] // rows,),
        in_specs=[
            pl.BlockSpec((rows, DL), lambda i: (i, 0)),
            pl.BlockSpec((1, DL), lambda i: (0, 0)),
        ],
        out_specs=pl.BlockSpec((rows, DL), lambda i: (i, 0)),
        compiler_params=pltpu.CompilerParams(vmem_limit_bytes=24 * MIB),
        cost_estimate=pl.CostEstimate(flops=8_000_000, bytes_accessed=5_300_000, transcendentals=256),
        name="norm_text",
    )(text, gain)


def per_device(
    frame_feats, selected, counts, video_start, queries, frame_pos, w_query, w_key, w_value, w_out,
    ln_gain, ln_bias, proj_weight, proj_bias, text_embeds, norm_gain,
):
    def move(x, target):
        return lax.ppermute(x, "tm", [(k, target(k)) for k in range(8)])

    def twin_of(device):
        return device ^ 1

    near_twin = move(proj_weight, crossing)
    twin = move(proj_weight, twin_of)
    parts = attend(
        selected, counts, video_start, frame_feats, frame_pos, queries, w_query, w_key, w_value
    )
    gain = norm_gain.reshape(1, DL)
    bias = proj_bias.reshape(1, DL)
    parts, text, share = lax.optimization_barrier((parts, text_embeds, proj_weight))
    far = move(near_twin, crossing)
    near = move(share, nearer)
    received = lax.all_to_all(parts, "video", split_axis=0, concat_axis=0, tiled=True)
    normed = norm_text(text, gain)
    ln_gain, ln_bias = ln_gain.reshape(1, WIDTH), ln_bias.reshape(1, WIDTH)
    received, normed, near, far, ln_gain, ln_bias, bias = lax.optimization_barrier(
        (received, normed, near, far, ln_gain, ln_bias, bias)
    )
    other_near_twin = move(near_twin, twin_of)
    other_near, far_twin = move(near, twin_of), move(far, twin_of)
    rows, wide, rest = merge(
        received, queries, w_out, ln_gain, ln_bias, video_start, bias, text_embeds,
        (proj_weight, twin, near_twin, other_near_twin, near, far),
    )
    rows, wide, rest, other_near, far_twin = lax.optimization_barrier((rows, wide, rest, other_near, far_twin))
    return place(rows, wide, rest, video_start, bias, gain, normed, (other_near, far_twin))


def solution(mesh):
    in_specs = (
        P("tm", "video", None, None), P("tm", None), P("tm"), P(), P(), P(), P(), P(), P(), P(),
        P(), P(), P(None, "tm"), P(), P(("tm", "video"), None), P(),
    )
    return jax.shard_map(
        per_device, mesh=mesh, in_specs=in_specs, out_specs=P(("tm", "video"), None), check_vma=False
    )
```

```python
import math

import jax
import jax.numpy as jnp
from jax import lax
from jax.experimental import pallas as pl
from jax.experimental.pallas import tpu as pltpu
from jax.sharding import PartitionSpec as P

HEADS = 12
HD = 64
WIDTH = HEADS * HD
VQ = 32
QF = 32
DL = 5120
SLOTS = 4
COLUMNS = 16
BLOCK = 256
SHARE = DL // 8
WINDOW = 48
STATS = 128
CHUNK = 8
NEAR = 6
MERGE_VMEM = 66_100_000
GROUP = 4
NEG = -1e30
MIB = 1 << 20

f32 = jnp.float32
bf16 = jnp.bfloat16


def iota(shape, axis):
    return lax.broadcasted_iota(jnp.int32, shape, axis)


def attend_kernel(
    selected_in, counts_in, starts_in, frames, pos_in, queries_in, w_query_in, w_key_in, w_value_in, out,
    selected, counts, starts, pos, queries, w_query, w_key, w_value, x_raw, x_keys, scores, values,
    folded, pos_wide, staged, scalar_sems, sems, weight_sems, out_sems,
):
    row = lax.axis_index("tm")
    column = lax.axis_index("video")
    scalars = [
        pltpu.make_async_copy(source, target, scalar_sems.at[i])
        for i, (source, target) in enumerate(
            ((selected_in, selected), (counts_in, counts), (starts_in, starts))
        )
    ]
    loads = [
        pltpu.make_async_copy(source, target, weight_sems.at[i])
        for i, (source, target) in enumerate((
            (queries_in, queries), (w_query_in, w_query), (w_key_in, w_key), (pos_in, pos),
            (w_value_in, w_value),
        ))
    ]
    for copy in scalars + loads:
        copy.start()
    for copy in scalars:
        copy.wait()

    def slot(video, j):
        count = counts[video]
        last = jnp.maximum(count >> 4, 1) - 1
        k = ((column * count) >> 4) + jnp.minimum(j, last)
        frame = selected[video, k] - column * 8
        live = (j <= last) & (frame >= 0) & (frame < 8)
        return k, jnp.clip(frame, 0, 7), live

    def fetch(video):
        for j in range(SLOTS):
            _, frame, _ = slot(video, j)
            pltpu.make_async_copy(
                frames.at[video, frame], x_raw.at[video * SLOTS + j], sems.at[video]
            ).start()

    pl.loop(0, COLUMNS)(fetch)
    for copy in loads[:2]:
        copy.wait()
    query = jnp.dot(queries[...], w_query[...], preferred_element_type=f32).astype(bf16)
    query = query * jnp.asarray(1.0 / math.sqrt(HD), bf16)
    loads[2].wait()
    for g in range(HEADS // GROUP):
        wide = GROUP * HD
        part = query[:, g * wide:(g + 1) * wide]
        part = jnp.concatenate([part] * GROUP, axis=0)
        same = iota(part.shape, 0) // VQ == iota(part.shape, 1) // HD
        part = jnp.where(same, part, jnp.zeros_like(part))
        fold = lax.dot_general(
            part, w_key[:, g * wide:(g + 1) * wide], (((1,), (1,)), ((), ())),
            preferred_element_type=f32,
        )
        rows = GROUP * VQ
        folded[g * rows:(g + 1) * rows, :] = fold.astype(bf16)
    loads[3].wait()
    pos_wide[...] = pos[...].astype(f32)

    lane = iota((VQ, STATS), 1)
    stat_head = lane % HEADS
    stat_part = lane // HEADS
    piece = stat_part % 3

    keys = SLOTS * QF

    def wait(chunk):
        for t in range(CHUNK):
            video = chunk * CHUNK + t
            pltpu.make_async_copy(
                frames.at[video, pl.ds(0, SLOTS)], x_raw.at[pl.ds(video * SLOTS, SLOTS)], sems.at[video]
            ).wait()

    def add(chunk, x_keys):
        for t in range(CHUNK):
            video = chunk * CHUNK + t
            for j in range(SLOTS):
                k, _, _ = slot(video, j)
                x = x_raw[video * SLOTS + j].astype(f32) + pos_wide[pl.ds(k, 1), :]
                at = (t * SLOTS + j) * QF
                x_keys[at:at + QF, :] = x.astype(bf16)

    def score(x_keys, scores, values):
        x = x_keys[...]
        scores[...] = lax.dot_general(folded[...], x, (((1,), (1,)), ((), ())), preferred_element_type=f32)
        values[...] = jnp.dot(x, w_value[...], preferred_element_type=f32).astype(bf16)

    def send(video):
        block = ((starts[row * COLUMNS + video] - row * (COLUMNS * BLOCK)) >> 8) & (COLUMNS - 1)
        return pltpu.make_async_copy(staged.at[video], out.at[block], out_sems.at[video])

    def finish(chunk, scores, values):
        for t in range(CHUNK):
            video = chunk * CHUNK + t
            alive = jnp.int32(0)
            for j in range(SLOTS):
                alive = alive + slot(video, j)[2].astype(jnp.int32)
            hidden = jnp.where(iota((1, keys), 1) < alive * QF, 0.0, NEG)
            s = scores[:, t * keys:(t + 1) * keys] + hidden
            top = jnp.max(s, axis=1, keepdims=True)
            p = jnp.exp(s - top)
            total = jnp.sum(p, axis=1, keepdims=True)
            p = p.astype(bf16)
            for g in range(HEADS // GROUP):
                wide = GROUP * HD
                rows = GROUP * VQ
                full = jnp.dot(
                    p[g * rows:(g + 1) * rows], values[t * keys:(t + 1) * keys, g * wide:(g + 1) * wide],
                    preferred_element_type=f32,
                )
                head = iota((VQ, wide), 1) // HD
                context = full[:VQ]
                for h in range(1, GROUP):
                    context = jnp.where(head == h, full[h * VQ:(h + 1) * VQ], context)
                staged[video, :, g * wide:(g + 1) * wide] = context.astype(bf16)
            stat = jnp.zeros((VQ, STATS), f32)
            for h in range(HEADS):
                one = jnp.where(stat_part < 3, top[h * VQ:(h + 1) * VQ], total[h * VQ:(h + 1) * VQ])
                stat = jnp.where(stat_head == h, one, stat)
            high = stat.astype(bf16).astype(f32)
            mid = (stat - high).astype(bf16).astype(f32)
            low = stat - high - mid
            stat = jnp.where(piece == 0, high, jnp.where(piece == 1, mid, low))
            stat = jnp.where(stat_part < 6, stat, 0.0)
            staged[video, :, WIDTH:] = stat.astype(bf16)

    chunks = COLUMNS // CHUNK
    wait(0)
    add(0, x_keys.at[0])
    loads[4].wait()
    for chunk in range(chunks + 1):
        if chunk + 1 < chunks:
            wait(chunk + 1)
        if chunk < chunks:
            score(x_keys.at[chunk % 2], scores.at[chunk % 2], values.at[chunk % 2])
        if chunk + 1 < chunks:
            add(chunk + 1, x_keys.at[(chunk + 1) % 2])
        if chunk > 0:
            finish(chunk - 1, scores.at[(chunk - 1) % 2], values.at[(chunk - 1) % 2])
        if chunk > 0:
            for t in range(CHUNK):
                send((chunk - 1) * CHUNK + t).start()
    for video in range(COLUMNS):
        send(video).wait()


def attend(selected, counts, starts, frames, pos, queries, w_query, w_key, w_value):
    return pl.pallas_call(
        attend_kernel,
        out_shape=jax.ShapeDtypeStruct((COLUMNS, VQ, WIDTH + STATS), bf16),
        in_specs=[pl.BlockSpec(memory_space=pl.ANY)] * 9,
        out_specs=pl.BlockSpec(memory_space=pl.ANY),
        scratch_shapes=[
            pltpu.SMEM(selected.shape, jnp.int32),
            pltpu.SMEM(counts.shape, jnp.int32),
            pltpu.SMEM(starts.shape, jnp.int32),
            pltpu.VMEM(pos.shape, bf16),
            pltpu.VMEM(queries.shape, bf16),
            pltpu.VMEM((WIDTH, WIDTH), bf16),
            pltpu.VMEM((WIDTH, WIDTH), bf16),
            pltpu.VMEM((WIDTH, WIDTH), bf16),
            pltpu.VMEM((COLUMNS * SLOTS, QF, WIDTH), bf16),
            pltpu.VMEM((2, CHUNK * SLOTS * QF, WIDTH), bf16),
            pltpu.VMEM((2, HEADS * VQ, CHUNK * SLOTS * QF), f32),
            pltpu.VMEM((2, CHUNK * SLOTS * QF, WIDTH), bf16),
            pltpu.VMEM((HEADS * VQ, WIDTH), bf16),
            pltpu.VMEM(pos.shape, f32),
            pltpu.VMEM((COLUMNS, VQ, WIDTH + STATS), bf16),
            pltpu.SemaphoreType.DMA((3,)),
            pltpu.SemaphoreType.DMA((COLUMNS,)),
            pltpu.SemaphoreType.DMA((5,)),
            pltpu.SemaphoreType.DMA((COLUMNS,)),
        ],
        compiler_params=pltpu.CompilerParams(vmem_limit_bytes=60 * MIB),
        cost_estimate=pl.CostEstimate(
            flops=9_000_000_000, bytes_accessed=8_000_000, transcendentals=800_000
        ),
        name="attend",
    )(selected, counts, starts, frames, pos, queries, w_query, w_key, w_value)


def nearer(device):
    return device ^ (2 + 4 * (device & 1))


def crossing(device):
    return device ^ (7 - 4 * (device & 1))


def blocks_of(device):
    twin = device ^ 1
    return (
        device, twin, nearer(device) ^ 1, nearer(twin) ^ 1, nearer(device), device ^ 4, nearer(twin), device ^ 5
    )


def window_of(starts):
    row = lax.axis_index("tm")
    column = lax.axis_index("video")
    first = (row * COLUMNS + column) * BLOCK
    offset = jnp.int32(0)
    for w in range(COLUMNS):
        at = starts[row * COLUMNS + w] - first
        offset = offset + jnp.where((at >= 0) & (at < BLOCK), at, 0)
    begin = pl.multiple_of(jnp.minimum(offset >> 4, (BLOCK - WINDOW) // 16) * 16, 16)
    return begin, offset - begin


def merge_kernel(
    parts_in, queries_in, w_out_in, gain_in, bias_in, starts_in, proj_bias_in, text, w0, w1, w2, w3, w4, w5,
    rows_out, wide_out, rest_out,
    parts, queries, w_out, gain, bias, starts, proj_bias, weights, window, sems, weight_sems,
):
    loads = [
        pltpu.make_async_copy(source, target, sems.at[i])
        for i, (source, target) in enumerate((
            (starts_in, starts), (parts_in, parts), (w_out_in, w_out), (queries_in, queries), (gain_in, gain),
            (bias_in, bias), (proj_bias_in, proj_bias),
        ))
    ]
    blocks = [
        pltpu.make_async_copy(source, weights.at[i], weight_sems.at[i])
        for i, source in enumerate((w0, w1, w2, w3, w4, w5))
    ]
    for copy in loads:
        copy.start()
    loads[0].wait()
    begin, shift = window_of(starts)
    fetch = pltpu.make_async_copy(text.at[pl.ds(begin, WINDOW)], window, sems.at[7])
    fetch.start()
    loads[1].wait()
    for copy in blocks:
        copy.start()
    stat = parts[:, :, WIDTH:].astype(f32).reshape(COLUMNS * VQ, STATS)

    def shifted(n):
        return pltpu.roll(stat, STATS - n * HEADS, 1)

    tops = stat + shifted(1) + shifted(2)
    totals = shifted(3) + shifted(4) + shifted(5)
    lane = iota((VQ, STATS), 1)
    real = lane < HEADS
    tops = [jnp.where(real, tops[c * VQ:(c + 1) * VQ], 0.0) for c in range(COLUMNS)]
    totals = [jnp.where(real, totals[c * VQ:(c + 1) * VQ], 1.0) for c in range(COLUMNS)]
    top = tops[0]
    for c in range(1, COLUMNS):
        top = jnp.maximum(top, tops[c])
    scales = [jnp.exp(t - top) for t in tops]
    total = scales[0] * totals[0]
    for c in range(1, COLUMNS):
        total = total + scales[c] * totals[c]
    inverse = jnp.where(real, 1.0 / total, 0.0)
    weight = jnp.concatenate([s * inverse for s in scales], axis=0)
    high = weight.astype(bf16)
    low = (weight - high.astype(f32)).astype(bf16)
    spread = (iota((2 * STATS, WIDTH), 0) % STATS == iota((2 * STATS, WIDTH), 1) // HD).astype(f32).astype(bf16)
    weight = jnp.dot(jnp.concatenate([high, low], axis=1), spread, preferred_element_type=f32)
    context = jnp.zeros((VQ, WIDTH), f32)
    for c in range(COLUMNS):
        context = context + weight[c * VQ:(c + 1) * VQ] * parts[c, :, :WIDTH].astype(f32)
    for copy in loads[2:]:
        copy.wait()
    residual = jnp.dot(context.astype(bf16), w_out[...], preferred_element_type=f32) + queries[...].astype(f32)
    mean = jnp.mean(residual, axis=-1, keepdims=True)
    centred = residual - mean
    variance = jnp.mean(centred * centred, axis=-1, keepdims=True)
    rows = (centred * lax.rsqrt(variance + 1e-12) * gain[...] + bias[...]).astype(bf16)
    pick = (iota((WINDOW, VQ), 0) - shift == iota((WINDOW, VQ), 1)).astype(f32).astype(bf16)
    rows = jnp.dot(pick, rows, preferred_element_type=f32).astype(bf16)
    rows_out[...] = rows
    place = iota((WINDOW, SHARE), 0) - shift
    inside = (place >= 0) & (place < VQ)
    fetch.wait()
    for i, block in enumerate(blocks_of(lax.axis_index("tm"))):
        here = pl.ds(pl.multiple_of(block * SHARE, 128), SHARE)
        text_rows = window[:, here]
        if i < NEAR:
            blocks[i].wait()
            result = jnp.dot(rows, weights[i], preferred_element_type=f32) + proj_bias[:, here]
            wide_out[:, i * SHARE:(i + 1) * SHARE] = jnp.where(
                inside, result, text_rows.astype(f32)
            ).astype(bf16)
        else:
            rest_out[:, (i - NEAR) * SHARE:(i - NEAR + 1) * SHARE] = text_rows


def merge(parts, queries, w_out, gain, bias, starts, proj_bias, text, weights):
    vmem = pl.BlockSpec(memory_space=pltpu.VMEM)
    anywhere = pl.BlockSpec(memory_space=pl.ANY)
    return pl.pallas_call(
        merge_kernel,
        out_shape=[
            jax.ShapeDtypeStruct((WINDOW, WIDTH), bf16),
            jax.ShapeDtypeStruct((WINDOW, NEAR * SHARE), bf16),
            jax.ShapeDtypeStruct((WINDOW, DL - NEAR * SHARE), bf16),
        ],
        in_specs=[anywhere] * 14,
        out_specs=[vmem, vmem, vmem],
        scratch_shapes=[
            pltpu.VMEM(parts.shape, bf16),
            pltpu.VMEM(queries.shape, bf16),
            pltpu.VMEM((WIDTH, WIDTH), bf16),
            pltpu.VMEM((1, WIDTH), f32),
            pltpu.VMEM((1, WIDTH), f32),
            pltpu.SMEM(starts.shape, jnp.int32),
            pltpu.VMEM((1, DL), f32),
            pltpu.VMEM((NEAR, WIDTH, SHARE), bf16),
            pltpu.VMEM((WINDOW, DL), bf16),
            pltpu.SemaphoreType.DMA((8,)),
            pltpu.SemaphoreType.DMA((NEAR,)),
        ],
        compiler_params=pltpu.CompilerParams(vmem_limit_bytes=MERGE_VMEM),
        cost_estimate=pl.CostEstimate(flops=500_000_000, bytes_accessed=9_000_000, transcendentals=70_000),
        name="merge",
    )(parts, queries, w_out, gain, bias, starts, proj_bias, text, *weights)


def place_kernel(
    rows_in, wide_in, rest_in, starts_in, proj_bias_in, norm_gain_in, normed, w6, w7, done,
    starts, proj_bias, norm_gain, weights, wide, done_rows, sems, weight_sems,
):
    loads = [
        pltpu.make_async_copy(source, target, sems.at[i])
        for i, (source, target) in enumerate((
            (starts_in, starts), (proj_bias_in, proj_bias), (norm_gain_in, norm_gain),
        ))
    ]
    blocks = [
        pltpu.make_async_copy(source, weights.at[i], weight_sems.at[i]) for i, source in enumerate((w6, w7))
    ]
    for copy in loads + blocks:
        copy.start()
    rows = rows_in[...]
    squares = jnp.zeros((WINDOW, 1), f32)
    all_blocks = blocks_of(lax.axis_index("tm"))
    for i, block in enumerate(all_blocks):
        here = pl.ds(pl.multiple_of(block * SHARE, 128), SHARE)
        if i < NEAR:
            embeds = wide_in[:, i * SHARE:(i + 1) * SHARE].astype(f32)
        else:
            if i == NEAR:
                loads[0].wait()
                begin, shift = window_of(starts)
                place = iota((WINDOW, SHARE), 0) - shift
                inside = (place >= 0) & (place < VQ)
                loads[1].wait()
            blocks[i - NEAR].wait()
            result = jnp.dot(rows, weights[i - NEAR], preferred_element_type=f32) + proj_bias[:, here]
            text_rows = rest_in[:, (i - NEAR) * SHARE:(i - NEAR + 1) * SHARE]
            embeds = jnp.where(inside, result, text_rows.astype(f32)).astype(bf16).astype(f32)
        wide[:, i * SHARE:(i + 1) * SHARE] = embeds
        squares = squares + jnp.sum(embeds * embeds, axis=-1, keepdims=True)
    scale = lax.rsqrt(squares * (1.0 / DL) + 1e-05)
    loads[2].wait()
    stores = []
    for i, block in enumerate(all_blocks):
        here = pl.ds(pl.multiple_of(block * SHARE, 128), SHARE)
        done_rows[:, here] = (wide[:, i * SHARE:(i + 1) * SHARE] * scale * norm_gain[:, here]).astype(bf16)
        store = pltpu.make_async_copy(
            done_rows.at[:, here], done.at[pl.ds(begin, WINDOW), here], sems.at[3 + i]
        )
        store.start()
        stores.append(store)
    for store in stores:
        store.wait()


def place(rows, wide, rest, starts, proj_bias, norm_gain, normed, weights):
    vmem = pl.BlockSpec(memory_space=pltpu.VMEM)
    anywhere = pl.BlockSpec(memory_space=pl.ANY)
    return pl.pallas_call(
        place_kernel,
        out_shape=jax.ShapeDtypeStruct(normed.shape, bf16),
        in_specs=[vmem] * 3 + [anywhere] * 6,
        out_specs=anywhere,
        input_output_aliases={6: 0},
        scratch_shapes=[
            pltpu.SMEM(starts.shape, jnp.int32),
            pltpu.VMEM((1, DL), f32),
            pltpu.VMEM((1, DL), f32),
            pltpu.VMEM((8 - NEAR, WIDTH, SHARE), bf16),
            pltpu.VMEM((WINDOW, DL), f32),
            pltpu.VMEM((WINDOW, DL), bf16),
            pltpu.SemaphoreType.DMA((11,)),
            pltpu.SemaphoreType.DMA((8 - NEAR,)),
        ],
        compiler_params=pltpu.CompilerParams(vmem_limit_bytes=MERGE_VMEM),
        name="place",
    )(rows, wide, rest, starts, proj_bias, norm_gain, normed, *weights)


def norm_rows(wide, gain):
    squares = jnp.mean(wide * wide, axis=-1, keepdims=True)
    return (wide * lax.rsqrt(squares + 1e-05) * gain).astype(bf16)


def text_kernel(text, gain, out):
    out[...] = norm_rows(text[...].astype(f32), gain[...])


def norm_text(text, gain):
    rows = 64
    return pl.pallas_call(
        text_kernel,
        out_shape=jax.ShapeDtypeStruct(text.shape, bf16),
        grid=(text.shape[0] // rows,),
        in_specs=[
            pl.BlockSpec((rows, DL), lambda i: (i, 0)),
            pl.BlockSpec((1, DL), lambda i: (0, 0)),
        ],
        out_specs=pl.BlockSpec((rows, DL), lambda i: (i, 0)),
        compiler_params=pltpu.CompilerParams(vmem_limit_bytes=24 * MIB),
        cost_estimate=pl.CostEstimate(flops=8_000_000, bytes_accessed=5_300_000, transcendentals=256),
        name="norm_text",
    )(text, gain)


def per_device(
    frame_feats, selected, counts, video_start, queries, frame_pos, w_query, w_key, w_value, w_out,
    ln_gain, ln_bias, proj_weight, proj_bias, text_embeds, norm_gain,
):
    def move(x, target):
        return lax.ppermute(x, "tm", [(k, target(k)) for k in range(8)])

    def twin_of(device):
        return device ^ 1

    near_twin = move(proj_weight, crossing)
    twin = move(proj_weight, twin_of)
    parts = attend(
        selected, counts, video_start, frame_feats, frame_pos, queries, w_query, w_key, w_value
    )
    gain = norm_gain.reshape(1, DL)
    bias = proj_bias.reshape(1, DL)
    parts, text, share = lax.optimization_barrier((parts, text_embeds, proj_weight))
    far = move(near_twin, crossing)
    near = move(share, nearer)
    received = lax.all_to_all(parts, "video", split_axis=0, concat_axis=0, tiled=True)
    normed = norm_text(text, gain)
    ln_gain, ln_bias = ln_gain.reshape(1, WIDTH), ln_bias.reshape(1, WIDTH)
    received, normed, near, far, ln_gain, ln_bias, bias = lax.optimization_barrier(
        (received, normed, near, far, ln_gain, ln_bias, bias)
    )
    other_near_twin = move(near_twin, twin_of)
    other_near, far_twin = move(near, twin_of), move(far, twin_of)
    rows, wide, rest = merge(
        received, queries, w_out, ln_gain, ln_bias, video_start, bias, text_embeds,
        (proj_weight, twin, near_twin, other_near_twin, near, far),
    )
    rows, wide, rest, other_near, far_twin = lax.optimization_barrier((rows, wide, rest, other_near, far_twin))
    return place(rows, wide, rest, video_start, bias, gain, normed, (other_near, far_twin))


def solution(mesh):
    in_specs = (
        P("tm", "video", None, None), P("tm", None), P("tm"), P(), P(), P(), P(), P(), P(), P(),
        P(), P(), P(None, "tm"), P(), P(("tm", "video"), None), P(),
    )
    return jax.shard_map(
        per_device, mesh=mesh, in_specs=in_specs, out_specs=P(("tm", "video"), None), check_vma=False
    )
```
